32 devices in a mesh: len: 16 (over z, x, core), dep: 2 (over y).
Axes of the slice: x: 2, y: 2, z: 4, core: 2. Of those that a mesh axis runs over, the one named last changes fastest.
Arguments:
- forward_states: bfloat16 [3, 19, 128, 16, 256], P(None, None, 'len', 'dep'), may hold values from 0 to 1, as said below
- adjoint_end: float32 [19, 128, 16, 256], P(None, 'len', 'dep'), may hold values from -6 to 6
- cell_kind: int32 [128, 16, 256], P('len', 'dep'), may hold values from 0 to 2
- basis_len: float32 [128, 64], P('len'), may hold values from -1 to 1
- basis_dep: float32 [16, 64], P('dep'), may hold values from -3 to 3
- basis_span: float32 [256, 32], replicated, may hold values from -0.75 to 0.75
Outputs:
- adjoint_start: float32 [19, 128, 16, 256], P(None, 'len', 'dep')
- coefficients: float32 [64, 64, 32], P('len', 'dep')
The draws below stay inside these ranges and needn't reach their ends.
Inputs may be any that keep to these rules, and one draw needn't show every extreme that they name: `forward_states`: every population is positive and each cell's populations sum to between 0.5 and 1.6.
All inputs are finite; a program needn't handle non-finite values.
Results may differ from the reference program's by a relative error of at most 0.0003.
Values sent between devices are 32-bit elements; how exact they have to be, the bound alone decides.
A program may use at most 64 MiB of HBM per device.

```python
import jax
import jax.numpy as jnp
from jax import lax

STEPS = 3
MX = 64
MY = 64
MZ = 32
NX = 128
NY = 16
NZ = 256


velocities = [(0, 0, 0), (1, 0, 0), (-1, 0, 0), (0, 1, 0), (0, -1, 0), (0, 0, 1), (0, 0, -1), (1, 1, 0), (-1, -1, 0), (1, -1, 0), (-1, 1, 0), (1, 0, 1), (-1, 0, -1), (1, 0, -1), (-1, 0, 1), (0, 1, 1), (0, -1, -1), (0, 1, -1), (0, -1, 1)]


def lattice_weight_drawn(vel):
    total = abs(vel[0]) + abs(vel[1]) + abs(vel[2])
    return 1.0 / 3.0 if total == 0 else 1.0 / 18.0 if total == 1 else 1.0 / 36.0


def draw_forward_states(key, part):
    key = jax.random.fold_in(key, 11)
    key_rho, key_vel, key_eps = jax.random.split(key, 3)
    shape = (STEPS, NX, NY, NZ)
    rho = jax.random.uniform(key_rho, shape, jnp.float32, 0.9, 1.1)
    speed = jnp.clip(0.05 * jax.random.normal(key_vel, (3,) + shape, jnp.float32), -0.12, 0.12)
    noise = jax.random.uniform(key_eps, (STEPS, 19, NX, NY, NZ), jnp.float32, -0.3, 0.3)
    usq = speed[0] * speed[0] + speed[1] * speed[1] + speed[2] * speed[2]
    pops = []
    for i, vel in enumerate(velocities):
        along = vel[0] * speed[0] + vel[1] * speed[1] + vel[2] * speed[2]
        feq = lattice_weight_drawn(vel) * rho * (1.0 + 3.0 * along + 4.5 * along * along - 1.5 * usq)
        pops.append(feq * (1.0 + noise[:, i]))
    return jnp.stack(pops, axis=1).astype(jnp.bfloat16)


def set_ends(array, key, least, top_value):
    longest = array.shape.index(max(array.shape))
    spots = []
    for shift in (0, 1):
        where = [jax.random.randint(jax.random.fold_in(key, axis), (), 0, length) for axis, length in enumerate(array.shape)]
        where[longest] = (where[longest] + shift) % array.shape[longest]
        spots.append(tuple(where))
    return array.at[spots[0]].set(least).at[spots[1]].set(top_value)


def shard_levels(rng, extent, cuts, low, top_value):
    factor_of = 1.0
    for dim, shards_of in cuts:
        draws = jax.random.uniform(jax.random.fold_in(jax.random.fold_in(rng, 6), dim), (shards_of,), jnp.float32, low / len(cuts), top_value / len(cuts))
        factor_of = factor_of * jnp.repeat(jnp.exp(draws), extent[dim] // shards_of).reshape((-1,) + (1,) * (len(extent) - 1 - dim))
    return factor_of


def normal_values(rng, extent, scale, limit, cuts=(), held_as=jnp.bfloat16):
    gain = shard_levels(rng, extent, cuts, -0.22, 0.18) if cuts else 1.0
    entries = jax.random.normal(rng, extent, jnp.float32) * scale * gain
    return jnp.minimum(jnp.maximum(entries, -limit), limit).astype(held_as)


def setup_inputs(seed: int = 0) -> dict:
    key_list = jax.random.split(jax.random.key(seed), 7)
    forward_states = draw_forward_states(jax.random.fold_in(key_list[6], 71), 0)
    adjoint_end = normal_values(key_list[1], (19, NX, NY, NZ), 1.0, 6.0, ((1, 16), (2, 2)), jnp.float32)
    cell_kind = set_ends(jax.random.randint(key_list[2], (NX, NY, NZ), 0, 3), jax.random.fold_in(key_list[2], 1), 0, 2).astype(jnp.int32)
    basis_len = normal_values(key_list[3], (NX, MX), (NX // 4) ** -0.5, 1.0, ((0, 16),), jnp.float32)
    basis_dep = normal_values(key_list[4], (NY, MY), (NY // 4) ** -0.5, 3.0, ((0, 2),), jnp.float32)
    basis_span = normal_values(key_list[5], (NZ, MZ), (NZ // 4) ** -0.5, 0.75, (), jnp.float32)
    return dict(forward_states=forward_states, adjoint_end=adjoint_end, cell_kind=cell_kind, basis_len=basis_len, basis_dep=basis_dep, basis_span=basis_span)


velocities = [(0, 0, 0), (1, 0, 0), (-1, 0, 0), (0, 1, 0), (0, -1, 0), (0, 0, 1), (0, 0, -1),
              (1, 1, 0), (-1, -1, 0), (1, -1, 0), (-1, 1, 0), (1, 0, 1), (-1, 0, -1), (1, 0, -1),
              (-1, 0, 1), (0, 1, 1), (0, -1, -1), (0, 1, -1), (0, -1, 1)]
opposite = [0, 2, 1, 4, 3, 6, 5, 8, 7, 10, 9, 12, 11, 14, 13, 16, 15, 18, 17]
omega = 1.25


def lattice_weight(vel):
    total = abs(vel[0]) + abs(vel[1]) + abs(vel[2])
    return 1.0 / 3.0 if total == 0 else (1.0 / 18.0 if total == 1 else 1.0 / 36.0)


def collide_back(post, forward, kind):
    fwd = forward.astype(jnp.float32)
    rho = jnp.sum(fwd, axis=0)
    moment = [sum(float(vel[d]) * fwd[i] for i, vel in enumerate(velocities) if vel[d] != 0) for d in range(3)]
    speed = [moment[d] / rho for d in range(3)]
    usq = speed[0] * speed[0] + speed[1] * speed[1] + speed[2] * speed[2]
    acc_rho = jnp.zeros_like(rho)
    acc_mom = [jnp.zeros_like(rho) for d in range(3)]
    sens = jnp.zeros_like(rho)
    for i, vel in enumerate(velocities):
        weight = lattice_weight(vel)
        along = sum(float(vel[d]) * speed[d] for d in range(3) if vel[d] != 0) if i > 0 else jnp.zeros_like(rho)
        feq = weight * rho * (1.0 + 3.0 * along + 4.5 * along * along - 1.5 * usq)
        sens = sens + post[i] * (feq - fwd[i])
        weighted = weight * post[i]
        acc_rho = acc_rho + weighted * (1.0 - 4.5 * along * along + 1.5 * usq)
        for d in range(3):
            acc_mom[d] = acc_mom[d] + weighted * (3.0 * vel[d] + 9.0 * along * vel[d] - 3.0 * speed[d])
    solid = kind == 2
    result = []
    for j, vel in enumerate(velocities):
        grad = acc_rho
        for d in range(3):
            if vel[d] != 0:
                grad = grad + float(vel[d]) * acc_mom[d]
        fluid_value = (1.0 - omega) * post[j] + omega * grad
        result.append(jnp.where(solid, post[opposite[j]], fluid_value))
    return jnp.stack(result), jnp.where(solid, 0.0, sens)


def reference(forward_states, adjoint_end, cell_kind, basis_len, basis_dep, basis_span):
    adjoint = adjoint_end
    surface = (cell_kind == 1).astype(jnp.float32)
    sens_total = jnp.zeros(cell_kind.shape, jnp.float32)
    for step in range(STEPS - 1, -1, -1):
        pulled = []
        for i, vel in enumerate(velocities):
            moved = jnp.roll(adjoint[i], (-vel[0], -vel[1], -vel[2]), axis=(0, 1, 2))
            if vel[0] != 0:
                moved = moved + 2.0 * vel[0] * surface
            pulled.append(moved)
        post = jnp.stack(pulled)
        adjoint, sens = collide_back(post, forward_states[step], cell_kind)
        sens_total = sens_total + sens
    nx, ny, nz = sens_total.shape
    span_part = jnp.dot(sens_total.reshape(nx * ny, nz), basis_span, preferred_element_type=jnp.float32,
                        precision=lax.Precision.HIGHEST).reshape(nx, ny, -1)
    depth_part = jnp.einsum("xyr,yq->xqr", span_part, basis_dep, precision=lax.Precision.HIGHEST)
    coefficients = jnp.einsum("xqr,xp->pqr", depth_part, basis_len, precision=lax.Precision.HIGHEST)
    return adjoint, coefficients
```

```python
import functools

import jax
import jax.numpy as jnp
from jax import lax
from jax.experimental import pallas as pl
from jax.experimental.pallas import tpu as pltpu
from jax.sharding import PartitionSpec as P

STEPS = 3
MESH = pl.DeviceIdType.MESH

velocities = [
    (0, 0, 0),
    (1, 0, 0),
    (-1, 0, 0),
    (0, 1, 0),
    (0, -1, 0),
    (0, 0, 1),
    (0, 0, -1),
    (1, 1, 0),
    (-1, -1, 0),
    (1, -1, 0),
    (-1, 1, 0),
    (1, 0, 1),
    (-1, 0, -1),
    (1, 0, -1),
    (-1, 0, 1),
    (0, 1, 1),
    (0, -1, -1),
    (0, 1, -1),
    (0, -1, 1),
]
omega = 1.25
COUNT = len(velocities)
PAIRS = [(i, i + 1) for i in range(1, COUNT, 2)]
ORDER = (
    [i for i, v in enumerate(velocities) if v[0] == 1]
    + [i for i, v in enumerate(velocities) if v[0] == -1]
    + [i for i, v in enumerate(velocities) if v[0] == 0]
)
PLACE = {i: k for k, i in enumerate(ORDER)}
SIGNS = (1, -1)
Y_POPS = [[i for i, v in enumerate(velocities) if v[1] == sign] for sign in SIGNS]
CORNERS = [i for i, v in enumerate(velocities) if v[0] != 0 and v[1] != 0]


def exact_dot(a, b, dims=((1,), (0,))):
    return lax.dot_general(
        a,
        b,
        (dims, ((), ())),
        precision=lax.Precision.HIGHEST,
        preferred_element_type=jnp.float32,
    )


def one_hot(shape, test):
    rows = lax.broadcasted_iota(jnp.int32, shape, 0)
    cols = lax.broadcasted_iota(jnp.int32, shape, 1)
    return jnp.where(test(rows, cols), 1.0, 0.0)


def kernel(
    sizes,
    fwd_hbm,
    adj_hbm,
    kind_ref,
    len_ref,
    dep_ref,
    span_ref,
    out_ref,
    coef_ref,
    adj,
    fwd,
    gap,
    speeds,
    ysend,
    yhalo,
    csend,
    chalo,
    sens,
    tbuf,
    tgot,
    rgot,
    depgot,
    span_wide,
    len_wide,
    load_sem,
    fwd_sem,
    x_sems,
    y_sems,
    c_sems,
    t_sems,
    r_sems,
    b_sems,
):
    count_len, count_dep, nx, ny, nz, mx, my, mz = sizes
    at_len = lax.axis_index("len")
    at_dep = lax.axis_index("dep")
    own_p, own_q = mx // count_len, my // count_dep
    fold = 128 // mz
    highs = ny // fold
    piece = tbuf.shape[1]

    def device(shift_len, shift_dep):
        return (
            lax.rem(at_len + (shift_len % count_len), count_len),
            lax.rem(at_dep + (shift_dep % count_dep), count_dep),
        )

    loads = [
        pltpu.make_async_copy(adj_hbm.at[i], adj.at[0, k, pl.ds(1, nx)], load_sem)
        for k, i in enumerate(ORDER)
    ]
    for copy in loads:
        copy.start()
    fwd_loads = [
        pltpu.make_async_copy(fwd_hbm.at[t], fwd.at[t], fwd_sem.at[t]) for t in range(STEPS)
    ]
    for t in range(STEPS - 1, -1, -1):
        fwd_loads[t].start()

    peers = {(k, 0) for k in range(1, count_len)} | {(0, k) for k in range(1, count_dep)}
    peers |= {(a % count_len, b % count_dep) for a in SIGNS for b in SIGNS}
    barrier = pltpu.get_barrier_semaphore()
    for peer in sorted(peers):
        pl.semaphore_signal(barrier, inc=1, device_id=device(*peer), device_id_type=MESH)

    def remote(src, dst, sems, index, target):
        return pltpu.make_async_remote_copy(
            src_ref=src,
            dst_ref=dst,
            send_sem=sems.at[(0,) + index],
            recv_sem=sems.at[(1,) + index],
            device_id=target,
            device_id_type=MESH,
        )

    def halo_copies(step):
        x_copies, y_copies, c_copies = [], [], []
        for side, sign in enumerate(SIGNS):
            pops = pl.ds(5 * side, 5)
            x_copies.append(
                remote(
                    adj.at[step, pops, 1 if sign == 1 else nx],
                    adj.at[step, pops, nx + 1 if sign == 1 else 0],
                    x_sems,
                    (step, side),
                    device(-sign, 0),
                )
            )
            y_copies.append(
                remote(
                    ysend.at[step, side],
                    yhalo.at[step, side],
                    y_sems,
                    (step, side),
                    device(0, -sign),
                )
            )
        for k, i in enumerate(CORNERS):
            vel = velocities[i]
            c_copies.append(
                remote(
                    csend.at[step, k],
                    chalo.at[step, k],
                    c_sems,
                    (step, k),
                    device(-vel[0], -vel[1]),
                )
            )
        return x_copies, y_copies, c_copies

    def fill_corners(step):
        for k, i in enumerate(CORNERS):
            vel = velocities[i]
            side = SIGNS.index(vel[1])
            row = 0 if vel[0] == 1 else nx - 1
            csend[step, k] = ysend[step, side, Y_POPS[side].index(i), pl.ds(row, 1), :]

    def fill_rows(step, i, x, value):
        vel = velocities[i]
        if vel[1] != 0:
            side = SIGNS.index(vel[1])
            row = value[0:1, :] if vel[1] == 1 else value[ny - 1 : ny, :]
            ysend[step, side, Y_POPS[side].index(i), pl.ds(x, 1), :] = row

    copies = [halo_copies(step) for step in range(STEPS)]

    def send(step):
        for group in copies[step]:
            for copy in group:
                copy.start()

    pltpu.make_async_copy(adj_hbm, adj.at[0, :, pl.ds(1, nx)], load_sem).wait()

    def first_rows(x, carry):
        for pops in Y_POPS:
            for i in pops:
                fill_rows(0, i, x, adj[0, PLACE[i], x + 1])
        return carry

    lax.fori_loop(0, nx, first_rows, 0)
    fill_corners(0)
    pl.semaphore_wait(barrier, len(peers))
    send(0)
    basis_copies = [
        remote(dep_ref, depgot.at[k], b_sems, (k,), device(0, k)) for k in range(1, count_dep)
    ]
    for copy in basis_copies:
        copy.start()

    def prepare(t):
        def plane(x, carry):
            f = [fwd[t, i, x].astype(jnp.float32) for i in range(COUNT)]
            sums = [f[i] + f[o] for i, o in PAIRS]
            difs = [f[i] - f[o] for i, o in PAIRS]
            rho = f[0]
            for part in sums:
                rho = rho + part
            inverse = 1.0 / rho
            speed = []
            for d in range(3):
                moment = None
                for (i, o), dif in zip(PAIRS, difs):
                    c = velocities[i][d]
                    if c != 0:
                        if moment is None:
                            moment = dif
                        else:
                            moment = moment + dif if c > 0 else moment - dif
                speed.append(moment * inverse)
                speeds[t, d, x] = speed[d]
            usq = speed[0] * speed[0] + speed[1] * speed[1] + speed[2] * speed[2]
            base = rho * (1.0 - 1.5 * usq)
            gap[t, 0, x] = (1.0 / 3.0) * base - f[0]
            for i, o in PAIRS:
                vel = velocities[i]
                terms = [(speed[d], vel[d]) for d in range(3) if vel[d] != 0]
                along = terms[0][0]
                if len(terms) == 2:
                    along = along + terms[1][0] if terms[1][1] > 0 else along - terms[1][0]
                weight = 1.0 / 18.0 if len(terms) == 1 else 1.0 / 36.0
                mass = weight * rho * along
                even = weight * base + 4.5 * mass * along
                odd = 3.0 * mass
                gap[t, i, x] = even + odd - f[i]
                gap[t, o, x] = even - odd - f[o]
            return carry

        fwd_loads[t].wait()
        lax.fori_loop(0, nx, plane, 0)

    rows_of = lax.broadcasted_iota(jnp.int32, (ny, nz), 0)

    def collide(step, x, edge):
        t = STEPS - 1 - step
        kind = kind_ref[x]
        solid = kind == 2
        push = jnp.where(kind == 1, 2.0, 0.0)
        post = []
        for i, vel in enumerate(velocities):
            value = adj[step, PLACE[i], x + (1 + vel[0])]
            if vel[1] != 0:
                side = SIGNS.index(vel[1])
                j = Y_POPS[side].index(i)
                if vel[0] != 0 and edge:
                    at = x + vel[0]
                    inside = (at >= 0) & (at < nx)
                    near = yhalo[step, side, j, pl.ds(jnp.clip(at, 0, nx - 1), 1), :]
                    row = jnp.where(inside, near, chalo[step, CORNERS.index(i)])
                else:
                    row = yhalo[step, side, j, pl.ds(x + vel[0], 1), :]
                if vel[1] == 1:
                    value = jnp.where(rows_of == ny - 1, row, pltpu.roll(value, ny - 1, 0))
                else:
                    value = jnp.where(rows_of == 0, row, pltpu.roll(value, 1, 0))
            if vel[2] != 0:
                value = pltpu.roll(value, (-vel[2]) % nz, 1)
            if vel[0] == 1:
                value = value + push
            elif vel[0] == -1:
                value = value - push
            post.append(value)

        change = post[0] * gap[t, 0, x]
        for i in range(1, COUNT):
            change = change + post[i] * gap[t, i, x]
        where = pl.ds(pl.multiple_of(x * ny, ny), ny)
        if step == 0:
            sens[where, :] = change
        elif step < STEPS - 1:
            sens[where, :] = sens[where, :] + change
        else:
            sens[where, :] = jnp.where(solid, 0.0, sens[where, :] + change)

        s = {i: post[i] + post[o] for i, o in PAIRS}
        d = {i: post[i] - post[o] for i, o in PAIRS}
        ux, uy, uz = (speeds[t, k, x] for k in range(3))
        xy, xz, yz = s[7] + s[9], s[11] + s[13], s[15] + s[17]
        sx, sy, sz = 2.0 * s[1], 2.0 * s[3], 2.0 * s[5]
        m0 = 12.0 * post[0] + (sx + sy + sz) + (xy + xz + yz)
        mxx, myy, mzz = sx + xy + xz, sy + xy + yz, sz + xz + yz
        mxy, mxz, myz = s[7] - s[9], s[11] - s[13], s[15] - s[17]
        m1x = 2.0 * d[1] + (d[7] + d[9]) + (d[11] + d[13])
        m1y = 2.0 * d[3] + (d[7] - d[9]) + (d[15] + d[17])
        m1z = 2.0 * d[5] + (d[11] - d[13]) + (d[15] - d[17])
        bx = mxx * ux + mxy * uy + mxz * uz
        by = mxy * ux + myy * uy + myz * uz
        bz = mxz * ux + myz * uy + mzz * uz
        usq = ux * ux + uy * uy + uz * uz
        along = ux * bx + uy * by + uz * bz
        acc_rho = (omega / 36.0) * (m0 * (1.0 + 1.5 * usq) - 4.5 * along)
        acc = [
            (omega / 12.0) * (m + 3.0 * b - u * m0)
            for m, b, u in ((m1x, bx, ux), (m1y, by, uy), (m1z, bz, uz))
        ]

        def store(i, value):
            if step == STEPS - 1:
                out_ref[i, x] = value
            else:
                adj[step + 1, PLACE[i], x + 1] = value
                fill_rows(step + 1, i, x, value)

        store(0, jnp.where(solid, post[0], (1.0 - omega) * post[0] + acc_rho))
        for i, o in PAIRS:
            vel = velocities[i]
            terms = [(acc[k], vel[k]) for k in range(3) if vel[k] != 0]
            grad = terms[0][0]
            if len(terms) == 2:
                grad = grad + terms[1][0] if terms[1][1] > 0 else grad - terms[1][0]
            store(i, jnp.where(solid, post[o], (1.0 - omega) * post[i] + (acc_rho + grad)))
            store(o, jnp.where(solid, post[i], (1.0 - omega) * post[o] + (acc_rho - grad)))

    prepare(STEPS - 1)
    spread = one_hot((mz, 128), lambda r, c: lax.rem(c, mz) == r)
    span_wide[...] = exact_dot(span_ref[...], spread)
    total = count_len * piece
    pick = one_hot(
        (total, mx),
        lambda r, c: (lax.div(r, piece) * own_p + lax.div(lax.rem(r, piece), highs) == c)
        & (lax.rem(r, piece) < own_p * highs),
    )
    lens = exact_dot(pick, len_ref[...], ((1,), (1,)))
    cells = one_hot((nx, nx * ny), lambda r, c: lax.div(c, ny) == r)
    halves = one_hot(
        (total, nx * ny),
        lambda r, c: lax.div(lax.rem(c, ny), fold) == lax.rem(lax.rem(r, piece), highs),
    )
    len_wide[...] = exact_dot(lens, cells) * halves

    for step in range(STEPS):
        x_copies, y_copies, c_copies = copies[step]
        for copy in y_copies:
            copy.wait_recv()

        def inner(x, carry):
            collide(step, x, False)
            return carry

        lax.fori_loop(1, nx - 1, inner, 0)
        for copy in x_copies + c_copies:
            copy.wait_recv()

        def outer(k, carry):
            collide(step, k * (nx - 1), True)
            return carry

        lax.fori_loop(0, 2, outer, 0)
        if step < STEPS - 1:
            fill_corners(step + 1)
            send(step + 1)
            prepare(STEPS - 2 - step)

    narrow = exact_dot(sens[...], span_wide[...])
    keep = one_hot(
        (nx * ny, 128), lambda r, c: lax.rem(lax.rem(r, ny), fold) == lax.div(c, mz)
    )
    partial = exact_dot(len_wide[...], narrow * keep)
    tbuf[...] = partial.reshape(tbuf.shape)
    t_copies = [
        remote(tbuf.at[device(k, 0)[0]], tgot.at[k], t_sems, (k,), device(k, 0))
        for k in range(1, count_len)
    ]
    for copy in t_copies:
        copy.start()

    for copy in basis_copies:
        copy.wait_recv()
    width = fold * piece
    mine = one_hot(
        (own_p * own_q, my), lambda r, c: lax.rem(r, own_q) + at_dep * own_q == c
    )
    lay = one_hot(
        (ny, width),
        lambda r, c: lax.rem(lax.rem(c, piece), highs) * fold + lax.div(c, piece) == r,
    )
    match = one_hot(
        (own_p * own_q, width),
        lambda r, c: lax.div(lax.rem(c, piece), highs) == lax.div(r, own_q),
    )
    deps = [
        exact_dot(
            exact_dot(mine, dep_ref[...] if k == 0 else depgot[k], ((1,), (1,))), lay
        )
        * match
        for k in range(count_dep)
    ]

    reduced = tbuf[at_len]
    for k in range(1, count_len):
        t_copies[k - 1].wait_recv()
        reduced = reduced + tgot[k]
    rgot[0] = reduced
    r_copies = [
        remote(rgot.at[0], rgot.at[k], r_sems, (k,), device(0, k)) for k in range(1, count_dep)
    ]
    for copy in r_copies:
        copy.start()

    def depth_modes(k):
        held = rgot[k]
        tall = jnp.concatenate(
            [held if j == 0 else pltpu.roll(held, 128 - j * mz, 1) for j in range(fold)], axis=0
        )
        return exact_dot(deps[k], tall)

    modes = depth_modes(0)
    for k in range(1, count_dep):
        r_copies[k - 1].wait_recv()
        modes = modes + depth_modes(k)
    coef_ref[...] = modes[:, :mz].reshape(coef_ref.shape)

    for step in range(STEPS):
        for group in copies[step]:
            for copy in group:
                copy.wait_send()
    for copy in basis_copies + t_copies + r_copies:
        copy.wait_send()


def on_device(forward_states, adjoint_end, cell_kind, basis_len, basis_dep, basis_span):
    count_len = lax.axis_size("len")
    count_dep = lax.axis_size("dep")
    nx, ny, nz = cell_kind.shape
    mx, my, mz = basis_len.shape[1], basis_dep.shape[1], basis_span.shape[1]
    sizes = (count_len, count_dep, nx, ny, nz, mx, my, mz)
    own_p = mx // count_len
    highs = ny // (128 // mz)
    piece = -(-own_p * highs // 8) * 8
    f32 = jnp.float32
    dma = pltpu.SemaphoreType.DMA
    vmem = pl.BlockSpec(memory_space=pltpu.VMEM)
    hbm = pl.BlockSpec(memory_space=pl.ANY)
    return pl.pallas_call(
        functools.partial(kernel, sizes),
        out_shape=(
            jax.ShapeDtypeStruct((COUNT, nx, ny, nz), f32),
            jax.ShapeDtypeStruct((own_p, my // count_dep, mz), f32),
        ),
        in_specs=[hbm, hbm, vmem, vmem, vmem, vmem],
        out_specs=(vmem, vmem),
        scratch_shapes=[
            pltpu.VMEM((STEPS, COUNT, nx + 2, ny, nz), f32),
            pltpu.VMEM(forward_states.shape, forward_states.dtype),
            pltpu.VMEM((STEPS, COUNT, nx, ny, nz), f32),
            pltpu.VMEM((STEPS, 3, nx, ny, nz), f32),
            pltpu.VMEM((STEPS, 2, 5, nx, nz), f32),
            pltpu.VMEM((STEPS, 2, 5, nx, nz), f32),
            pltpu.VMEM((STEPS, 4, 1, nz), f32),
            pltpu.VMEM((STEPS, 4, 1, nz), f32),
            pltpu.VMEM((nx * ny, nz), f32),
            pltpu.VMEM((count_len, piece, 128), f32),
            pltpu.VMEM((count_len, piece, 128), f32),
            pltpu.VMEM((count_dep, piece, 128), f32),
            pltpu.VMEM((count_dep, ny, my), f32),
            pltpu.VMEM((nz, 128), f32),
            pltpu.VMEM((count_len * piece, nx * ny), f32),
            dma,
            dma((STEPS,)),
            dma((2, STEPS, 2)),
            dma((2, STEPS, 2)),
            dma((2, STEPS, 4)),
            dma((2, count_len)),
            dma((2, count_dep)),
            dma((2, count_dep)),
        ],
        compiler_params=pltpu.CompilerParams(
            collective_id=0, has_side_effects=True, vmem_limit_bytes=48 * 1024 * 1024
        ),
        cost_estimate=pl.CostEstimate(
            flops=STEPS * 600 * nx * ny * nz, bytes_accessed=5 * 1024 * 1024, transcendentals=0
        ),
    )(forward_states, adjoint_end, cell_kind, basis_len, basis_dep, basis_span)


def solution(mesh):
    return jax.shard_map(
        on_device,
        mesh=mesh,
        in_specs=(
            P(None, None, "len", "dep", None),
            P(None, "len", "dep", None),
            P("len", "dep", None),
            P("len", None),
            P("dep", None),
            P(),
        ),
        out_specs=(P(None, "len", "dep", None), P("len", "dep", None)),
        check_vma=False,
    )
```

```python
import functools

import jax
import jax.numpy as jnp
from jax import lax
from jax.experimental import pallas as pl
from jax.experimental.pallas import tpu as pltpu
from jax.sharding import PartitionSpec as P

STEPS = 3
MESH = pl.DeviceIdType.MESH

velocities = [
    (0, 0, 0),
    (1, 0, 0),
    (-1, 0, 0),
    (0, 1, 0),
    (0, -1, 0),
    (0, 0, 1),
    (0, 0, -1),
    (1, 1, 0),
    (-1, -1, 0),
    (1, -1, 0),
    (-1, 1, 0),
    (1, 0, 1),
    (-1, 0, -1),
    (1, 0, -1),
    (-1, 0, 1),
    (0, 1, 1),
    (0, -1, -1),
    (0, 1, -1),
    (0, -1, 1),
]
omega = 1.25
COUNT = len(velocities)
PAIRS = [(i, i + 1) for i in range(1, COUNT, 2)]
ORDER = (
    [i for i, v in enumerate(velocities) if v[0] == 1]
    + [i for i, v in enumerate(velocities) if v[0] == -1]
    + [i for i, v in enumerate(velocities) if v[0] == 0]
)
PLACE = {i: k for k, i in enumerate(ORDER)}
SIGNS = (1, -1)
Y_POPS = [[i for i, v in enumerate(velocities) if v[1] == sign] for sign in SIGNS]
CORNERS = [i for i, v in enumerate(velocities) if v[0] != 0 and v[1] != 0]


def exact_dot(a, b, dims=((1,), (0,))):
    return lax.dot_general(
        a,
        b,
        (dims, ((), ())),
        precision=lax.Precision.HIGHEST,
        preferred_element_type=jnp.float32,
    )


def quotient(a, n):
    return a >> (n.bit_length() - 1) if n & (n - 1) == 0 else lax.div(a, n)


def remainder(a, n):
    return a & (n - 1) if n & (n - 1) == 0 else lax.rem(a, n)


def one_hot(shape, test):
    rows = lax.broadcasted_iota(jnp.int32, shape, 0)
    cols = lax.broadcasted_iota(jnp.int32, shape, 1)
    return jnp.where(test(rows, cols), 1.0, 0.0)


def kernel(
    sizes,
    fwd_hbm,
    adj_hbm,
    kind_hbm,
    len_hbm,
    dep_hbm,
    span_hbm,
    out_hbm,
    coef_ref,
    adj,
    fwd,
    gap,
    speeds,
    ysend,
    yhalo,
    csend,
    chalo,
    sens,
    tbuf,
    tgot,
    rgot,
    depgot,
    span_wide,
    len_wide,
    kind_ref,
    len_ref,
    dep_ref,
    span_ref,
    out_ref,
    load_sem,
    fwd_sem,
    small_sem,
    out_sem,
    x_sems,
    y_sems,
    c_sems,
    t_sems,
    r_sems,
    b_sems,
):
    count_len, count_dep, nx, ny, nz, mx, my, mz = sizes
    at_len = lax.axis_index("len")
    at_dep = lax.axis_index("dep")
    own_p, own_q = mx // count_len, my // count_dep
    fold = 128 // mz
    highs = ny // fold
    piece = tbuf.shape[1]

    def device(shift_len, shift_dep):
        return (
            lax.rem(at_len + (shift_len % count_len), count_len),
            lax.rem(at_dep + (shift_dep % count_dep), count_dep),
        )

    loads = [
        pltpu.make_async_copy(adj_hbm.at[i], adj.at[0, k, pl.ds(1, nx)], load_sem)
        for k, i in enumerate(ORDER)
    ]
    for copy in loads:
        copy.start()
    small = [
        pltpu.make_async_copy(src, dst, small_sem.at[k])
        for k, (src, dst) in enumerate(
            ((dep_hbm, dep_ref), (kind_hbm, kind_ref), (len_hbm, len_ref), (span_hbm, span_ref))
        )
    ]
    for copy in small:
        copy.start()
    fwd_loads = [
        pltpu.make_async_copy(fwd_hbm.at[t], fwd.at[t], fwd_sem.at[t]) for t in range(STEPS)
    ]
    for t in range(STEPS - 1, -1, -1):
        fwd_loads[t].start()

    peers = {(k, 0) for k in range(1, count_len)} | {(0, k) for k in range(1, count_dep)}
    peers |= {(a % count_len, b % count_dep) for a in SIGNS for b in SIGNS}
    barrier = pltpu.get_barrier_semaphore()
    for peer in sorted(peers):
        pl.semaphore_signal(barrier, inc=1, device_id=device(*peer), device_id_type=MESH)

    def remote(src, dst, sems, index, target):
        return pltpu.make_async_remote_copy(
            src_ref=src,
            dst_ref=dst,
            send_sem=sems.at[(0,) + index],
            recv_sem=sems.at[(1,) + index],
            device_id=target,
            device_id_type=MESH,
        )

    def halo_copies(step):
        x_copies, y_copies, c_copies = [], [], []
        for side, sign in enumerate(SIGNS):
            pops = pl.ds(5 * side, 5)
            x_copies.append(
                remote(
                    adj.at[step, pops, 1 if sign == 1 else nx],
                    adj.at[step, pops, nx + 1 if sign == 1 else 0],
                    x_sems,
                    (step, side),
                    device(-sign, 0),
                )
            )
            y_copies.append(
                remote(
                    ysend.at[step, side],
                    yhalo.at[step, side],
                    y_sems,
                    (step, side),
                    device(0, -sign),
                )
            )
        for k, i in enumerate(CORNERS):
            vel = velocities[i]
            c_copies.append(
                remote(
                    csend.at[step, k],
                    chalo.at[step, k],
                    c_sems,
                    (step, k),
                    device(-vel[0], -vel[1]),
                )
            )
        return x_copies, y_copies, c_copies

    def fill_corners(step):
        for k, i in enumerate(CORNERS):
            vel = velocities[i]
            side = SIGNS.index(vel[1])
            row = 0 if vel[0] == 1 else nx - 1
            csend[step, k] = ysend[step, side, Y_POPS[side].index(i), pl.ds(row, 1), :]

    def fill_rows(step, i, x, value):
        vel = velocities[i]
        if vel[1] != 0:
            side = SIGNS.index(vel[1])
            row = value[0:1, :] if vel[1] == 1 else value[ny - 1 : ny, :]
            ysend[step, side, Y_POPS[side].index(i), pl.ds(x, 1), :] = row

    copies = [halo_copies(step) for step in range(STEPS)]

    def send(step):
        for group in copies[step]:
            for copy in group:
                copy.start()

    pltpu.make_async_copy(adj_hbm, adj.at[0, :, pl.ds(1, nx)], load_sem).wait()

    def first_rows(x, carry):
        for pops in Y_POPS:
            for i in pops:
                fill_rows(0, i, x, adj[0, PLACE[i], x + 1])
        return carry

    lax.fori_loop(0, nx, first_rows, 0)
    fill_corners(0)
    pl.semaphore_wait(barrier, len(peers))
    send(0)
    for copy in small:
        copy.wait()
    basis_copies = [
        remote(dep_ref, depgot.at[k], b_sems, (k,), device(0, k)) for k in range(1, count_dep)
    ]
    for copy in basis_copies:
        copy.start()

    def prepare(t):
        def plane(x, carry):
            f = [fwd[t, i, x].astype(jnp.float32) for i in range(COUNT)]
            sums = [f[i] + f[o] for i, o in PAIRS]
            difs = [f[i] - f[o] for i, o in PAIRS]
            rho = f[0]
            for part in sums:
                rho = rho + part
            inverse = 1.0 / rho
            speed = []
            for d in range(3):
                moment = None
                for (i, o), dif in zip(PAIRS, difs):
                    c = velocities[i][d]
                    if c != 0:
                        if moment is None:
                            moment = dif
                        else:
                            moment = moment + dif if c > 0 else moment - dif
                speed.append(moment * inverse)
                speeds[t, d, x] = speed[d]
            usq = speed[0] * speed[0] + speed[1] * speed[1] + speed[2] * speed[2]
            base = rho * (1.0 - 1.5 * usq)
            gap[t, 0, x] = (1.0 / 3.0) * base - f[0]
            for i, o in PAIRS:
                vel = velocities[i]
                terms = [(speed[d], vel[d]) for d in range(3) if vel[d] != 0]
                along = terms[0][0]
                if len(terms) == 2:
                    along = along + terms[1][0] if terms[1][1] > 0 else along - terms[1][0]
                weight = 1.0 / 18.0 if len(terms) == 1 else 1.0 / 36.0
                mass = weight * rho * along
                even = weight * base + 4.5 * mass * along
                odd = 3.0 * mass
                gap[t, i, x] = even + odd - f[i]
                gap[t, o, x] = even - odd - f[o]
            return carry

        fwd_loads[t].wait()
        lax.fori_loop(0, nx, plane, 0)

    rows_of = lax.broadcasted_iota(jnp.int32, (ny, nz), 0)

    def collide(step, x, edge):
        t = STEPS - 1 - step
        kind = kind_ref[x]
        solid = kind == 2
        push = jnp.where(kind == 1, 2.0, 0.0)
        post = []
        for i, vel in enumerate(velocities):
            value = adj[step, PLACE[i], x + (1 + vel[0])]
            if vel[1] != 0:
                side = SIGNS.index(vel[1])
                j = Y_POPS[side].index(i)
                if vel[0] != 0 and edge:
                    at = x + vel[0]
                    inside = (at >= 0) & (at < nx)
                    near = yhalo[step, side, j, pl.ds(jnp.clip(at, 0, nx - 1), 1), :]
                    row = jnp.where(inside, near, chalo[step, CORNERS.index(i)])
                else:
                    row = yhalo[step, side, j, pl.ds(x + vel[0], 1), :]
                if vel[1] == 1:
                    value = jnp.where(rows_of == ny - 1, row, pltpu.roll(value, ny - 1, 0))
                else:
                    value = jnp.where(rows_of == 0, row, pltpu.roll(value, 1, 0))
            if vel[2] != 0:
                value = pltpu.roll(value, (-vel[2]) % nz, 1)
            if vel[0] == 1:
                value = value + push
            elif vel[0] == -1:
                value = value - push
            post.append(value)

        change = post[0] * gap[t, 0, x]
        for i in range(1, COUNT):
            change = change + post[i] * gap[t, i, x]
        where = pl.ds(pl.multiple_of(x * ny, ny), ny)
        if step == 0:
            sens[where, :] = change
        elif step < STEPS - 1:
            sens[where, :] = sens[where, :] + change
        else:
            sens[where, :] = jnp.where(solid, 0.0, sens[where, :] + change)

        s = {i: post[i] + post[o] for i, o in PAIRS}
        d = {i: post[i] - post[o] for i, o in PAIRS}
        ux, uy, uz = (speeds[t, k, x] for k in range(3))
        xy, xz, yz = s[7] + s[9], s[11] + s[13], s[15] + s[17]
        sx, sy, sz = 2.0 * s[1], 2.0 * s[3], 2.0 * s[5]
        m0 = 12.0 * post[0] + (sx + sy + sz) + (xy + xz + yz)
        mxx, myy, mzz = sx + xy + xz, sy + xy + yz, sz + xz + yz
        mxy, mxz, myz = s[7] - s[9], s[11] - s[13], s[15] - s[17]
        m1x = 2.0 * d[1] + (d[7] + d[9]) + (d[11] + d[13])
        m1y = 2.0 * d[3] + (d[7] - d[9]) + (d[15] + d[17])
        m1z = 2.0 * d[5] + (d[11] - d[13]) + (d[15] - d[17])
        bx = mxx * ux + mxy * uy + mxz * uz
        by = mxy * ux + myy * uy + myz * uz
        bz = mxz * ux + myz * uy + mzz * uz
        usq = ux * ux + uy * uy + uz * uz
        along = ux * bx + uy * by + uz * bz
        acc_rho = (omega / 36.0) * (m0 * (1.0 + 1.5 * usq) - 4.5 * along)
        acc = [
            (omega / 12.0) * (m + 3.0 * b - u * m0)
            for m, b, u in ((m1x, bx, ux), (m1y, by, uy), (m1z, bz, uz))
        ]

        def store(i, value):
            if step == STEPS - 1:
                out_ref[i, x] = value
            else:
                adj[step + 1, PLACE[i], x + 1] = value
                fill_rows(step + 1, i, x, value)

        store(0, jnp.where(solid, post[0], (1.0 - omega) * post[0] + acc_rho))
        for i, o in PAIRS:
            vel = velocities[i]
            terms = [(acc[k], vel[k]) for k in range(3) if vel[k] != 0]
            grad = terms[0][0]
            if len(terms) == 2:
                grad = grad + terms[1][0] if terms[1][1] > 0 else grad - terms[1][0]
            store(i, jnp.where(solid, post[o], (1.0 - omega) * post[i] + (acc_rho + grad)))
            store(o, jnp.where(solid, post[i], (1.0 - omega) * post[o] + (acc_rho - grad)))

    prepare(STEPS - 1)
    spread = one_hot((mz, 128), lambda r, c: remainder(c, mz) == r)
    span_wide[...] = exact_dot(span_ref[...], spread, ((0,), (0,)))
    total = count_len * piece
    pick = one_hot(
        (total, mx),
        lambda r, c: (quotient(r, piece) * own_p + quotient(remainder(r, piece), highs) == c)
        & (remainder(r, piece) < own_p * highs),
    )
    lens = exact_dot(pick, len_ref[...], ((1,), (1,)))
    cells = one_hot((nx, nx * ny), lambda r, c: quotient(c, ny) == r)
    halves = one_hot(
        (total, nx * ny),
        lambda r, c: quotient(remainder(c, ny), fold) == remainder(remainder(r, piece), highs),
    )
    len_wide[...] = exact_dot(lens, cells) * halves

    for step in range(STEPS):
        x_copies, y_copies, c_copies = copies[step]
        for copy in y_copies:
            copy.wait_recv()

        def inner(x, carry):
            collide(step, x, False)
            return carry

        lax.fori_loop(1, nx - 1, inner, 0)
        for copy in x_copies + c_copies:
            copy.wait_recv()

        def outer(k, carry):
            collide(step, k * (nx - 1), True)
            return carry

        lax.fori_loop(0, 2, outer, 0)
        if step < STEPS - 1:
            fill_corners(step + 1)
            send(step + 1)
            prepare(STEPS - 2 - step)

    narrow = exact_dot(sens[...], span_wide[...])
    keep = one_hot(
        (nx * ny, 128), lambda r, c: remainder(remainder(r, ny), fold) == quotient(c, mz)
    )
    partial = exact_dot(len_wide[...], narrow * keep)
    tbuf[...] = partial.reshape(tbuf.shape)
    t_copies = [
        remote(tbuf.at[device(k, 0)[0]], tgot.at[k], t_sems, (k,), device(k, 0))
        for k in range(1, count_len)
    ]
    for copy in t_copies:
        copy.start()
    out_copy = pltpu.make_async_copy(out_ref, out_hbm, out_sem)
    out_copy.start()

    for copy in basis_copies:
        copy.wait_recv()
    width = fold * piece
    mine = one_hot(
        (own_p * own_q, my), lambda r, c: remainder(r, own_q) + at_dep * own_q == c
    )
    lay = one_hot(
        (ny, width),
        lambda r, c: remainder(remainder(c, piece), highs) * fold + quotient(c, piece) == r,
    )
    match = one_hot(
        (own_p * own_q, width),
        lambda r, c: quotient(remainder(c, piece), highs) == quotient(r, own_q),
    )
    deps = [
        exact_dot(
            exact_dot(mine, dep_ref[...] if k == 0 else depgot[k], ((1,), (1,))), lay
        )
        * match
        for k in range(count_dep)
    ]

    reduced = tbuf[at_len]
    for k in range(1, count_len):
        t_copies[k - 1].wait_recv()
        reduced = reduced + tgot[k]
    rgot[0] = reduced
    r_copies = [
        remote(rgot.at[0], rgot.at[k], r_sems, (k,), device(0, k)) for k in range(1, count_dep)
    ]
    for copy in r_copies:
        copy.start()

    def depth_modes(k):
        held = rgot[k]
        tall = jnp.concatenate(
            [held if j == 0 else pltpu.roll(held, 128 - j * mz, 1) for j in range(fold)], axis=0
        )
        return exact_dot(deps[k], tall)

    modes = depth_modes(0)
    for k in range(1, count_dep):
        r_copies[k - 1].wait_recv()
        modes = modes + depth_modes(k)
    coef_ref[...] = modes[:, :mz].reshape(coef_ref.shape)

    for step in range(STEPS):
        for group in copies[step]:
            for copy in group:
                copy.wait_send()
    for copy in basis_copies + t_copies + r_copies:
        copy.wait_send()
    out_copy.wait()


def on_device(forward_states, adjoint_end, cell_kind, basis_len, basis_dep, basis_span):
    count_len = lax.axis_size("len")
    count_dep = lax.axis_size("dep")
    nx, ny, nz = cell_kind.shape
    mx, my, mz = basis_len.shape[1], basis_dep.shape[1], basis_span.shape[1]
    sizes = (count_len, count_dep, nx, ny, nz, mx, my, mz)
    own_p = mx // count_len
    highs = ny // (128 // mz)
    piece = -(-own_p * highs // 8) * 8
    f32 = jnp.float32
    dma = pltpu.SemaphoreType.DMA
    vmem = pl.BlockSpec(memory_space=pltpu.VMEM)
    hbm = pl.BlockSpec(memory_space=pl.ANY)
    return pl.pallas_call(
        functools.partial(kernel, sizes),
        out_shape=(
            jax.ShapeDtypeStruct((COUNT, nx, ny, nz), f32),
            jax.ShapeDtypeStruct((own_p, my // count_dep, mz), f32),
        ),
        in_specs=[hbm] * 6,
        out_specs=(hbm, vmem),
        scratch_shapes=[
            pltpu.VMEM((STEPS, COUNT, nx + 2, ny, nz), f32),
            pltpu.VMEM(forward_states.shape, forward_states.dtype),
            pltpu.VMEM((STEPS, COUNT, nx, ny, nz), f32),
            pltpu.VMEM((STEPS, 3, nx, ny, nz), f32),
            pltpu.VMEM((STEPS, 2, 5, nx, nz), f32),
            pltpu.VMEM((STEPS, 2, 5, nx, nz), f32),
            pltpu.VMEM((STEPS, 4, 1, nz), f32),
            pltpu.VMEM((STEPS, 4, 1, nz), f32),
            pltpu.VMEM((nx * ny, nz), f32),
            pltpu.VMEM((count_len, piece, 128), f32),
            pltpu.VMEM((count_len, piece, 128), f32),
            pltpu.VMEM((count_dep, piece, 128), f32),
            pltpu.VMEM((count_dep, ny, my), f32),
            pltpu.VMEM((nz, 128), f32),
            pltpu.VMEM((count_len * piece, nx * ny), f32),
            pltpu.VMEM(cell_kind.shape, cell_kind.dtype),
            pltpu.VMEM(basis_len.shape, f32),
            pltpu.VMEM(basis_dep.shape, f32),
            pltpu.VMEM((mz, nz), f32),
            pltpu.VMEM((COUNT, nx, ny, nz), f32),
            dma,
            dma((STEPS,)),
            dma((4,)),
            dma,
            dma((2, STEPS, 2)),
            dma((2, STEPS, 2)),
            dma((2, STEPS, 4)),
            dma((2, count_len)),
            dma((2, count_dep)),
            dma((2, count_dep)),
        ],
        compiler_params=pltpu.CompilerParams(
            collective_id=0, has_side_effects=True, vmem_limit_bytes=62 * 1024 * 1024
        ),
        cost_estimate=pl.CostEstimate(
            flops=STEPS * 600 * nx * ny * nz, bytes_accessed=5 * 1024 * 1024, transcendentals=0
        ),
    )(forward_states, adjoint_end, cell_kind, basis_len, basis_dep, basis_span.T)


def solution(mesh):
    return jax.shard_map(
        on_device,
        mesh=mesh,
        in_specs=(
            P(None, None, "len", "dep", None),
            P(None, "len", "dep", None),
            P("len", "dep", None),
            P("len", None),
            P("dep", None),
            P(),
        ),
        out_specs=(P(None, "len", "dep", None), P("len", "dep", None)),
        check_vma=False,
    )
```

```python
import functools

import jax
import jax.numpy as jnp
from jax import lax
from jax.experimental import pallas as pl
from jax.experimental.pallas import tpu as pltpu
from jax.sharding import PartitionSpec as P

STEPS = 3
MESH = pl.DeviceIdType.MESH

velocities = [
    (0, 0, 0),
    (1, 0, 0),
    (-1, 0, 0),
    (0, 1, 0),
    (0, -1, 0),
    (0, 0, 1),
    (0, 0, -1),
    (1, 1, 0),
    (-1, -1, 0),
    (1, -1, 0),
    (-1, 1, 0),
    (1, 0, 1),
    (-1, 0, -1),
    (1, 0, -1),
    (-1, 0, 1),
    (0, 1, 1),
    (0, -1, -1),
    (0, 1, -1),
    (0, -1, 1),
]
omega = 1.25
COUNT = len(velocities)
PAIRS = [(i, i + 1) for i in range(1, COUNT, 2)]
ORDER = (
    [i for i, v in enumerate(velocities) if v[0] == 1]
    + [i for i, v in enumerate(velocities) if v[0] == -1]
    + [i for i, v in enumerate(velocities) if v[0] == 0]
)
PLACE = {i: k for k, i in enumerate(ORDER)}
SIGNS = (1, -1)
Y_POPS = [[i for i, v in enumerate(velocities) if v[1] == sign] for sign in SIGNS]
CORNERS = [i for i, v in enumerate(velocities) if v[0] != 0 and v[1] != 0]


def exact_dot(a, b, dims=((1,), (0,))):
    return lax.dot_general(
        a,
        b,
        (dims, ((), ())),
        precision=lax.Precision.HIGHEST,
        preferred_element_type=jnp.float32,
    )


def quotient(a, n):
    return a >> (n.bit_length() - 1) if n & (n - 1) == 0 else lax.div(a, n)


def remainder(a, n):
    return a & (n - 1) if n & (n - 1) == 0 else lax.rem(a, n)


def one_hot(shape, test):
    rows = lax.broadcasted_iota(jnp.int32, shape, 0)
    cols = lax.broadcasted_iota(jnp.int32, shape, 1)
    return jnp.where(test(rows, cols), 1.0, 0.0)


def kernel(
    sizes,
    fwd_hbm,
    adj_hbm,
    kind_hbm,
    len_hbm,
    dep_hbm,
    span_hbm,
    out_hbm,
    coef_ref,
    adj,
    fwd,
    gap,
    speeds,
    ysend,
    yhalo,
    csend,
    chalo,
    sens,
    tbuf,
    tgot,
    rgot,
    depgot,
    span_wide,
    len_wide,
    kind_ref,
    len_ref,
    dep_ref,
    span_ref,
    out_ref,
    load_sem,
    fwd_sem,
    small_sem,
    out_sem,
    x_sems,
    y_sems,
    c_sems,
    t_sems,
    r_sems,
    b_sems,
):
    count_len, count_dep, nx, ny, nz, mx, my, mz = sizes
    at_len = lax.axis_index("len")
    at_dep = lax.axis_index("dep")
    own_p, own_q = mx // count_len, my // count_dep
    fold = 128 // mz
    highs = ny // fold
    piece = tbuf.shape[1]

    def device(shift_len, shift_dep):
        return (
            lax.rem(at_len + (shift_len % count_len), count_len),
            lax.rem(at_dep + (shift_dep % count_dep), count_dep),
        )

    loads = [
        pltpu.make_async_copy(adj_hbm.at[i], adj.at[0, k, pl.ds(1, nx)], load_sem)
        for k, i in enumerate(ORDER)
    ]
    for copy in loads:
        copy.start()
    small = [
        pltpu.make_async_copy(src, dst, small_sem.at[k])
        for k, (src, dst) in enumerate(
            ((dep_hbm, dep_ref), (kind_hbm, kind_ref), (len_hbm, len_ref), (span_hbm, span_ref))
        )
    ]
    for copy in small:
        copy.start()
    fwd_loads = [
        pltpu.make_async_copy(fwd_hbm.at[t], fwd.at[t], fwd_sem.at[t]) for t in range(STEPS)
    ]
    for t in range(STEPS - 1, -1, -1):
        fwd_loads[t].start()

    peers = {(k, 0) for k in range(1, count_len)} | {(0, k) for k in range(1, count_dep)}
    peers |= {(a % count_len, b % count_dep) for a in SIGNS for b in SIGNS}
    barrier = pltpu.get_barrier_semaphore()
    for peer in sorted(peers):
        pl.semaphore_signal(barrier, inc=1, device_id=device(*peer), device_id_type=MESH)

    def remote(src, dst, sems, index, target):
        return pltpu.make_async_remote_copy(
            src_ref=src,
            dst_ref=dst,
            send_sem=sems.at[(0,) + index],
            recv_sem=sems.at[(1,) + index],
            device_id=target,
            device_id_type=MESH,
        )

    def halo_copies(step):
        x_copies, y_copies, c_copies = [], [], []
        for side, sign in enumerate(SIGNS):
            pops = pl.ds(5 * side, 5)
            x_copies.append(
                remote(
                    adj.at[step, pops, 1 if sign == 1 else nx],
                    adj.at[step, pops, nx + 1 if sign == 1 else 0],
                    x_sems,
                    (step, side),
                    device(-sign, 0),
                )
            )
            y_copies.append(
                remote(
                    ysend.at[step, side],
                    yhalo.at[step, side],
                    y_sems,
                    (step, side),
                    device(0, -sign),
                )
            )
        for k, i in enumerate(CORNERS):
            vel = velocities[i]
            c_copies.append(
                remote(
                    csend.at[step, k],
                    chalo.at[step, k],
                    c_sems,
                    (step, k),
                    device(-vel[0], -vel[1]),
                )
            )
        return x_copies, y_copies, c_copies

    def fill_corners(step):
        for k, i in enumerate(CORNERS):
            vel = velocities[i]
            side = SIGNS.index(vel[1])
            row = 0 if vel[0] == 1 else nx - 1
            csend[step, k] = ysend[step, side, Y_POPS[side].index(i), pl.ds(row, 1), :]

    def fill_rows(step, i, x, value):
        vel = velocities[i]
        if vel[1] != 0:
            side = SIGNS.index(vel[1])
            row = value[0:1, :] if vel[1] == 1 else value[ny - 1 : ny, :]
            ysend[step, side, Y_POPS[side].index(i), pl.ds(x, 1), :] = row

    copies = [halo_copies(step) for step in range(STEPS)]

    def send(step):
        for group in copies[step]:
            for copy in group:
                copy.start()

    pltpu.make_async_copy(adj_hbm, adj.at[0, :, pl.ds(1, nx)], load_sem).wait()

    def first_rows(x, carry):
        for pops in Y_POPS:
            for i in pops:
                fill_rows(0, i, x, adj[0, PLACE[i], x + 1])
        return carry

    lax.fori_loop(0, nx, first_rows, 0)
    fill_corners(0)
    pl.semaphore_wait(barrier, len(peers))
    send(0)
    for copy in small:
        copy.wait()
    basis_copies = [
        remote(dep_ref, depgot.at[k], b_sems, (k,), device(0, k)) for k in range(1, count_dep)
    ]
    for copy in basis_copies:
        copy.start()

    def prepare(t):
        def plane(x, carry):
            f = [fwd[t, i, x].astype(jnp.float32) for i in range(COUNT)]
            sums = [f[i] + f[o] for i, o in PAIRS]
            difs = [f[i] - f[o] for i, o in PAIRS]
            rho = f[0]
            for part in sums:
                rho = rho + part
            inverse = 1.0 / rho
            speed = []
            for d in range(3):
                moment = None
                for (i, o), dif in zip(PAIRS, difs):
                    c = velocities[i][d]
                    if c != 0:
                        if moment is None:
                            moment = dif
                        else:
                            moment = moment + dif if c > 0 else moment - dif
                speed.append(moment * inverse)
                speeds[t, d, x] = speed[d]
            usq = speed[0] * speed[0] + speed[1] * speed[1] + speed[2] * speed[2]
            base = rho * (1.0 - 1.5 * usq)
            gap[t, 0, x] = (1.0 / 3.0) * base - f[0]
            for i, o in PAIRS:
                vel = velocities[i]
                terms = [(speed[d], vel[d]) for d in range(3) if vel[d] != 0]
                along = terms[0][0]
                if len(terms) == 2:
                    along = along + terms[1][0] if terms[1][1] > 0 else along - terms[1][0]
                weight = 1.0 / 18.0 if len(terms) == 1 else 1.0 / 36.0
                mass = weight * rho * along
                even = weight * base + 4.5 * mass * along
                odd = 3.0 * mass
                gap[t, i, x] = even + odd - f[i]
                gap[t, o, x] = even - odd - f[o]
            return carry

        fwd_loads[t].wait()
        lax.fori_loop(0, nx, plane, 0)

    rows_of = lax.broadcasted_iota(jnp.int32, (ny, nz), 0)

    def collide(step, x, edge):
        t = STEPS - 1 - step
        kind = kind_ref[x]
        solid = kind == 2
        push = jnp.where(kind == 1, 2.0, 0.0)
        post = []
        for i, vel in enumerate(velocities):
            value = adj[step, PLACE[i], x + (1 + vel[0])]
            if vel[1] != 0:
                side = SIGNS.index(vel[1])
                j = Y_POPS[side].index(i)
                if vel[0] != 0 and edge:
                    at = x + vel[0]
                    inside = (at >= 0) & (at < nx)
                    near = yhalo[step, side, j, pl.ds(jnp.clip(at, 0, nx - 1), 1), :]
                    row = jnp.where(inside, near, chalo[step, CORNERS.index(i)])
                else:
                    row = yhalo[step, side, j, pl.ds(x + vel[0], 1), :]
                if vel[1] == 1:
                    value = jnp.where(rows_of == ny - 1, row, pltpu.roll(value, ny - 1, 0))
                else:
                    value = jnp.where(rows_of == 0, row, pltpu.roll(value, 1, 0))
            if vel[2] != 0:
                value = pltpu.roll(value, (-vel[2]) % nz, 1)
            if vel[0] == 1:
                value = value + push
            elif vel[0] == -1:
                value = value - push
            post.append(value)

        change = post[0] * gap[t, 0, x]
        for i in range(1, COUNT):
            change = change + post[i] * gap[t, i, x]
        where = pl.ds(pl.multiple_of(x * ny, ny), ny)
        if step == 0:
            sens[where, :] = change
        elif step < STEPS - 1:
            sens[where, :] = sens[where, :] + change
        else:
            sens[where, :] = jnp.where(solid, 0.0, sens[where, :] + change)

        s = {i: post[i] + post[o] for i, o in PAIRS}
        d = {i: post[i] - post[o] for i, o in PAIRS}
        ux, uy, uz = (speeds[t, k, x] for k in range(3))
        xy, xz, yz = s[7] + s[9], s[11] + s[13], s[15] + s[17]
        sx, sy, sz = 2.0 * s[1], 2.0 * s[3], 2.0 * s[5]
        m0 = 12.0 * post[0] + (sx + sy + sz) + (xy + xz + yz)
        mxx, myy, mzz = sx + xy + xz, sy + xy + yz, sz + xz + yz
        mxy, mxz, myz = s[7] - s[9], s[11] - s[13], s[15] - s[17]
        m1x = 2.0 * d[1] + (d[7] + d[9]) + (d[11] + d[13])
        m1y = 2.0 * d[3] + (d[7] - d[9]) + (d[15] + d[17])
        m1z = 2.0 * d[5] + (d[11] - d[13]) + (d[15] - d[17])
        bx = mxx * ux + mxy * uy + mxz * uz
        by = mxy * ux + myy * uy + myz * uz
        bz = mxz * ux + myz * uy + mzz * uz
        usq = ux * ux + uy * uy + uz * uz
        along = ux * bx + uy * by + uz * bz
        acc_rho = (omega / 36.0) * (m0 * (1.0 + 1.5 * usq) - 4.5 * along)
        acc = [
            (omega / 12.0) * (m + 3.0 * b - u * m0)
            for m, b, u in ((m1x, bx, ux), (m1y, by, uy), (m1z, bz, uz))
        ]

        def store(i, value):
            if step == STEPS - 1:
                out_ref[i, x] = value
            else:
                adj[step + 1, PLACE[i], x + 1] = value
                fill_rows(step + 1, i, x, value)

        store(0, jnp.where(solid, post[0], (1.0 - omega) * post[0] + acc_rho))
        for i, o in PAIRS:
            vel = velocities[i]
            terms = [(acc[k], vel[k]) for k in range(3) if vel[k] != 0]
            grad = terms[0][0]
            if len(terms) == 2:
                grad = grad + terms[1][0] if terms[1][1] > 0 else grad - terms[1][0]
            store(i, jnp.where(solid, post[o], (1.0 - omega) * post[i] + (acc_rho + grad)))
            store(o, jnp.where(solid, post[i], (1.0 - omega) * post[o] + (acc_rho - grad)))

    prepare(STEPS - 1)
    spread = one_hot((mz, 128), lambda r, c: remainder(c, mz) == r)
    span_wide[...] = exact_dot(span_ref[...], spread, ((0,), (0,)))
    total = count_len * piece
    pick = one_hot(
        (total, mx),
        lambda r, c: (quotient(r, piece) * own_p + quotient(remainder(r, piece), highs) == c)
        & (remainder(r, piece) < own_p * highs),
    )
    lens = exact_dot(pick, len_ref[...], ((1,), (1,)))
    cells = one_hot((nx, nx * ny), lambda r, c: quotient(c, ny) == r)
    halves = one_hot(
        (total, nx * ny),
        lambda r, c: quotient(remainder(c, ny), fold) == remainder(remainder(r, piece), highs),
    )
    len_wide[...] = exact_dot(lens, cells) * halves

    for step in range(STEPS):
        x_copies, y_copies, c_copies = copies[step]
        for copy in y_copies:
            copy.wait_recv()

        def inner(x, carry):
            collide(step, x, False)
            return carry

        lax.fori_loop(1, nx - 1, inner, 0)
        for copy in x_copies + c_copies:
            copy.wait_recv()

        def outer(k, carry):
            collide(step, k * (nx - 1), True)
            return carry

        lax.fori_loop(0, 2, outer, 0)
        if step < STEPS - 1:
            fill_corners(step + 1)
            send(step + 1)
            prepare(STEPS - 2 - step)

    narrow = exact_dot(sens[...], span_wide[...])
    keep = one_hot(
        (nx * ny, 128), lambda r, c: remainder(remainder(r, ny), fold) == quotient(c, mz)
    )
    partial = exact_dot(len_wide[...], narrow * keep)
    tbuf[...] = partial.reshape(tbuf.shape)
    t_copies = [
        remote(tbuf.at[device(k, 0)[0]], tgot.at[k], t_sems, (k,), device(k, 0))
        for k in range(1, count_len)
    ]
    for copy in t_copies:
        copy.start()
    out_copy = pltpu.make_async_copy(out_ref, out_hbm, out_sem)
    out_copy.start()

    for copy in basis_copies:
        copy.wait_recv()
    width = fold * piece
    mine = one_hot(
        (own_p * own_q, my), lambda r, c: remainder(r, own_q) + at_dep * own_q == c
    )
    lay = one_hot(
        (ny, width),
        lambda r, c: remainder(remainder(c, piece), highs) * fold + quotient(c, piece) == r,
    )
    match = one_hot(
        (own_p * own_q, width),
        lambda r, c: quotient(remainder(c, piece), highs) == quotient(r, own_q),
    )
    deps = [
        exact_dot(
            exact_dot(mine, dep_ref[...] if k == 0 else depgot[k], ((1,), (1,))), lay
        )
        * match
        for k in range(count_dep)
    ]

    reduced = tbuf[at_len]
    for k in range(1, count_len):
        t_copies[k - 1].wait_recv()
        reduced = reduced + tgot[k]
    rgot[0] = reduced
    r_copies = [
        remote(rgot.at[0], rgot.at[k], r_sems, (k,), device(0, k)) for k in range(1, count_dep)
    ]
    for copy in r_copies:
        copy.start()

    def depth_modes(k):
        held = rgot[k]
        tall = jnp.concatenate(
            [held if j == 0 else pltpu.roll(held, 128 - j * mz, 1) for j in range(fold)], axis=0
        )
        return exact_dot(deps[k], tall)

    modes = depth_modes(0)
    for k in range(1, count_dep):
        r_copies[k - 1].wait_recv()
        modes = modes + depth_modes(k)
    coef_ref[...] = modes[:, :mz].reshape(coef_ref.shape)

    for step in range(STEPS):
        for group in copies[step]:
            for copy in group:
                copy.wait_send()
    for copy in basis_copies + t_copies + r_copies:
        copy.wait_send()
    out_copy.wait()


def hand_over(adj_in, coef_in, adj_out, coef_out, adj_held, coef_held, sems):
    parts = [(coef_in, coef_held, coef_out)]
    parts += [(adj_in.at[i], adj_held.at[i], adj_out.at[i]) for i in range(COUNT)]
    reads = [
        pltpu.make_async_copy(src, mid, sems.at[0, k]) for k, (src, mid, dst) in enumerate(parts)
    ]
    writes = [
        pltpu.make_async_copy(mid, dst, sems.at[1, k]) for k, (src, mid, dst) in enumerate(parts)
    ]
    for read in reads:
        read.start()
    for read, write in zip(reads, writes):
        read.wait()
        write.start()
    for write in writes:
        write.wait()


def on_device(forward_states, adjoint_end, cell_kind, basis_len, basis_dep, basis_span):
    count_len = lax.axis_size("len")
    count_dep = lax.axis_size("dep")
    nx, ny, nz = cell_kind.shape
    mx, my, mz = basis_len.shape[1], basis_dep.shape[1], basis_span.shape[1]
    sizes = (count_len, count_dep, nx, ny, nz, mx, my, mz)
    own_p = mx // count_len
    highs = ny // (128 // mz)
    piece = -(-own_p * highs // 8) * 8
    f32 = jnp.float32
    dma = pltpu.SemaphoreType.DMA
    vmem = pl.BlockSpec(memory_space=pltpu.VMEM)
    hbm = pl.BlockSpec(memory_space=pl.ANY)
    adjoint, coefficients = pl.pallas_call(
        functools.partial(kernel, sizes),
        out_shape=(
            jax.ShapeDtypeStruct((COUNT, nx, ny, nz), f32),
            jax.ShapeDtypeStruct((own_p, my // count_dep, mz), f32),
        ),
        in_specs=[hbm] * 6,
        out_specs=(hbm, vmem),
        scratch_shapes=[
            pltpu.VMEM((STEPS, COUNT, nx + 2, ny, nz), f32),
            pltpu.VMEM(forward_states.shape, forward_states.dtype),
            pltpu.VMEM((STEPS, COUNT, nx, ny, nz), f32),
            pltpu.VMEM((STEPS, 3, nx, ny, nz), f32),
            pltpu.VMEM((STEPS, 2, 5, nx, nz), f32),
            pltpu.VMEM((STEPS, 2, 5, nx, nz), f32),
            pltpu.VMEM((STEPS, 4, 1, nz), f32),
            pltpu.VMEM((STEPS, 4, 1, nz), f32),
            pltpu.VMEM((nx * ny, nz), f32),
            pltpu.VMEM((count_len, piece, 128), f32),
            pltpu.VMEM((count_len, piece, 128), f32),
            pltpu.VMEM((count_dep, piece, 128), f32),
            pltpu.VMEM((count_dep, ny, my), f32),
            pltpu.VMEM((nz, 128), f32),
            pltpu.VMEM((count_len * piece, nx * ny), f32),
            pltpu.VMEM(cell_kind.shape, cell_kind.dtype),
            pltpu.VMEM(basis_len.shape, f32),
            pltpu.VMEM(basis_dep.shape, f32),
            pltpu.VMEM((mz, nz), f32),
            pltpu.VMEM((COUNT, nx, ny, nz), f32),
            dma,
            dma((STEPS,)),
            dma((4,)),
            dma,
            dma((2, STEPS, 2)),
            dma((2, STEPS, 2)),
            dma((2, STEPS, 4)),
            dma((2, count_len)),
            dma((2, count_dep)),
            dma((2, count_dep)),
        ],
        compiler_params=pltpu.CompilerParams(
            collective_id=0, has_side_effects=True, vmem_limit_bytes=62 * 1024 * 1024
        ),
        cost_estimate=pl.CostEstimate(
            flops=STEPS * 600 * nx * ny * nz, bytes_accessed=5 * 1024 * 1024, transcendentals=0
        ),
    )(forward_states, adjoint_end, cell_kind, basis_len, basis_dep, basis_span.T)
    return pl.pallas_call(
        hand_over,
        out_shape=(
            jax.ShapeDtypeStruct(adjoint.shape, f32),
            jax.ShapeDtypeStruct(coefficients.shape, f32),
        ),
        in_specs=[hbm, hbm],
        out_specs=(hbm, hbm),
        scratch_shapes=[
            pltpu.VMEM(adjoint.shape, f32),
            pltpu.VMEM(coefficients.shape, f32),
            dma((2, COUNT + 1)),
        ],
        compiler_params=pltpu.CompilerParams(vmem_limit_bytes=62 * 1024 * 1024),
    )(adjoint, coefficients)


def solution(mesh):
    return jax.shard_map(
        on_device,
        mesh=mesh,
        in_specs=(
            P(None, None, "len", "dep", None),
            P(None, "len", "dep", None),
            P("len", "dep", None),
            P("len", None),
            P("dep", None),
            P(),
        ),
        out_specs=(P(None, "len", "dep", None), P("len", "dep", None)),
        check_vma=False,
    )
```
